32 devices in a mesh: zone: 2 (over y), tile: 16 (over z, x, core).
Axes of the slice: x: 2, y: 2, z: 4, core: 2. Of those that a mesh axis runs over, the one named last changes fastest.
Arguments:
- tiles: bfloat16 [96, 13, 256, 256], P(('zone', 'tile')), may hold values from -6 to 6
- seam_list: int32 [64], P(('zone', 'tile')), may hold values from 0 to 2, as said below
- source: int32 [768], P('zone'), may hold values from 0 to 47, as said below
- offsets: int32 [768, 2], P('zone'), may hold values from -2 to 2
- fractions: float32 [768, 2], P('zone'), may hold values from 0 to 1
- blend: float32 [768], P('zone'), may hold values from 0.25 to 0.75
Outputs:
- polar_blocks: bfloat16 [768, 13, 128, 128], P(('zone', 'tile'))
The draws below stay inside these ranges and needn't reach their ends.
Inputs may be any that keep to these rules, and one draw needn't show every extreme that they name: Within the blocks of one owner device, no source device (index v // 3 of the strip) supplies more than 3 blocks; in every draw each owner takes exactly 3 blocks from some source device. Source devices are unevenly popular. `seam_list`: the 2 entries of one device are distinct.
All inputs are finite; a program needn't handle non-finite values.
Results may differ from the reference program's by a relative error of at most 0.0062.
Values may be sent and summed in bfloat16 or wider, within the bound.
A program may use at most 192 MiB of HBM per device.

```python
import jax
import jax.numpy as jnp
from jax import lax

BANDS = 13
TR = 256
TC = 256
LOC = 3
OB = 24
SEAM_MAX = 2
CAP = 3
TILES = 96
BLOCKS = 768
N_ZONE = 2
N_TILE = 16
DEVICES = 32


def draw_seam_list(key, part):
    keys = jax.random.split(key, DEVICES)

    def pick(device_key):
        return jax.random.permutation(device_key, LOC)[:SEAM_MAX].astype(jnp.int32)
    return jax.vmap(pick)(keys).reshape(DEVICES * SEAM_MAX)


def draw_source(key, part):
    entries = N_TILE * CAP
    popular = jax.random.randint(jax.random.fold_in(key, 11), (N_ZONE, N_TILE), 0, 4)
    owner_keys = jax.random.split(jax.random.fold_in(key, 23), DEVICES)

    def owner(owner_key, owner_index):
        first_key, score_key, order_key, tile_key = jax.random.split(owner_key, 4)
        entry_ids = jnp.arange(entries, dtype=jnp.int32)
        entry_device = entry_ids // CAP
        favourite = jax.random.randint(first_key, (), 0, N_TILE)
        level = popular[owner_index // N_TILE][entry_device]
        score = jax.random.randint(score_key, (entries,), 0, 1024) + 1024 * level
        score = jnp.where(entry_device == favourite, -1, score)
        ranked = jnp.argsort(score * entries + entry_ids, stable=True)[:OB]
        chosen = entry_device[ranked]
        chosen = chosen[jax.random.permutation(order_key, OB)]
        local_tile = jax.random.randint(tile_key, (OB,), 0, LOC)
        return (chosen * LOC + local_tile).astype(jnp.int32)
    return jax.vmap(owner)(owner_keys, jnp.arange(DEVICES, dtype=jnp.int32)).reshape(DEVICES * OB)


def with_ends(array, stream_key, least, top_value):
    longest = array.shape.index(max(array.shape))
    spots = []
    for shift in (0, 1):
        where = [jax.random.randint(jax.random.fold_in(stream_key, axis), (), 0, length) for axis, length in enumerate(array.shape)]
        where[longest] = (where[longest] + shift) % array.shape[longest]
        spots.append(tuple(where))
    return array.at[spots[0]].set(least).at[spots[1]].set(top_value)


def steps_of(own_key, shape, shards, least, high):
    def one(position, parts):
        draws = jax.random.uniform(jax.random.fold_in(jax.random.fold_in(own_key, 6), position), (parts,), jnp.float32, least / len(shards), high / len(shards))
        return jnp.repeat(jnp.exp(draws), shape[position] // parts).reshape((-1,) + (1,) * (len(shape) - position - 1))

    gain = one(*shards[0])
    for cut in shards[1:]:
        gain = gain * one(*cut)
    return gain


def noise(rng, dims, scale, reach, shards=(), kind=jnp.bfloat16):
    factor_of = steps_of(rng, dims, shards, -0.22, 0.18) if shards else 1.0
    array = jax.random.normal(rng, dims, jnp.float32) * scale * factor_of
    return jnp.minimum(jnp.maximum(array, -reach), reach).astype(kind)


def setup_inputs(seed: int = 0) -> dict:
    streams_of = jax.random.split(jax.random.key(seed), 7)
    return {
        "tiles": noise(streams_of[0], (TILES, BANDS, TR, TC), 1.0, 6.0, ((0, 32),)),
        "seam_list": draw_seam_list(jax.random.fold_in(streams_of[6], 71), 0),
        "source": draw_source(jax.random.fold_in(streams_of[6], 71), 0),
        "offsets": with_ends(jax.random.randint(streams_of[3], (BLOCKS, 2), -2, 3), jax.random.fold_in(streams_of[3], 1), -2, 2).astype(jnp.int32),
        "fractions": jnp.clip(1.0 * jax.random.uniform(streams_of[4], (BLOCKS, 2), jnp.float32) ** steps_of(streams_of[4], (BLOCKS, 2), ((0, 2),), -0.2, 0.2), 0.0, 1.0),
        "blend": jnp.clip(0.25 + 0.5 * jax.random.uniform(streams_of[5], (BLOCKS,), jnp.float32) ** steps_of(streams_of[5], (BLOCKS,), ((0, 2),), -0.2, 0.2), 0.25, 0.75),
    }


def cubic_weight(dist):
    mag = jnp.abs(dist)
    near = (1.5 * mag - 2.5) * mag * mag + 1.0
    far = ((-0.5 * mag + 2.5) * mag - 4.0) * mag + 2.0
    return jnp.where(mag <= 1.0, near, jnp.where(mag < 2.0, far, jnp.zeros_like(mag)))


def kernel_matrix(out_len, in_len, shift):
    rows = jnp.arange(out_len, dtype=jnp.float32)[:, None]
    cols = jnp.arange(in_len, dtype=jnp.float32)[None, :]
    return cubic_weight(cols - (2.0 * rows + shift)).astype(jnp.bfloat16)


def resample(mixed, offset_pair, fraction_pair):
    height = mixed.shape[1]
    width = mixed.shape[2]
    row_kernel = kernel_matrix(height // 2, height, offset_pair[0].astype(jnp.float32) + fraction_pair[0])
    col_kernel = kernel_matrix(width // 2, width, offset_pair[1].astype(jnp.float32) + fraction_pair[1])
    across = jnp.einsum("bkt,ot->bko", mixed.astype(jnp.float32), col_kernel.astype(jnp.float32)).astype(jnp.bfloat16)
    result = jnp.einsum("ik,bko->bio", row_kernel.astype(jnp.float32), across.astype(jnp.float32))
    return result.astype(jnp.bfloat16)


def reference(tiles, seam_list, source, offsets, fractions, blend):
    row_tiles = N_TILE * LOC
    seams = seam_list.reshape(N_ZONE * N_TILE, SEAM_MAX)

    def single(index):
        zone_index = index // (N_TILE * OB)
        value = source[index]
        primary = tiles[zone_index * row_tiles + value]
        left_zone = jnp.maximum(zone_index - 1, 0)
        secondary = tiles[left_zone * row_tiles + value]
        listed = seams[left_zone * N_TILE + value // LOC]
        flagged = jnp.any(listed == value % LOC) & (zone_index > 0)
        weight = blend[index] * flagged.astype(jnp.float32)
        mixed = ((1.0 - weight) * primary.astype(jnp.float32) + weight * secondary.astype(jnp.float32)).astype(jnp.bfloat16)
        return resample(mixed, offsets[index], fractions[index])

    return lax.map(single, jnp.arange(BLOCKS, dtype=jnp.int32), batch_size=16)
```

```python
import functools

import jax
import jax.numpy as jnp
from jax import lax
from jax.experimental import pallas as pl
from jax.experimental.pallas import tpu as pltpu
from jax.sharding import PartitionSpec as P

lag = 2
MESH = pl.DeviceIdType.MESH


def line_length(count):
    best = 1
    for length in range(1, count + 1):
        if count % length == 0 and length * length <= count:
            best = length
    return best


def cubic_weight(dist):
    mag = jnp.abs(dist)
    near = (1.5 * mag - 2.5) * mag * mag + 1.0
    far = ((-0.5 * mag + 2.5) * mag - 4.0) * mag + 2.0
    return jnp.where(mag <= 1.0, near, jnp.where(mag < 2.0, far, jnp.zeros_like(mag)))


def exchange_kernel(
    sizes,
    prim_ref,
    sec_ref,
    weight_ref,
    shift_ref,
    tiles,
    planes,
    seams,
    incoming,
    row_k,
    col_k,
    plane_v,
    seam_v,
    out_v,
    z_send,
    z_recv,
    y_send,
    y_recv,
    x_send,
    x_recv,
    local_sem,
    own_sem,
):
    zones, line, groups, slots = sizes
    loc, bands, height, width = tiles.shape
    seam_count = seams.shape[2]
    zone = lax.axis_index("zone")
    myself = lax.axis_index("tile")
    place = myself // groups
    group = myself % groups

    def device(zone_at, place_at, group_at):
        return (zone_at, place_at * groups + group_at)

    has_up = place + 1 < line
    has_down = place >= 1
    has_next = zone + 1 < zones
    has_left = zone >= 1

    barrier = pltpu.get_barrier_semaphore()

    def greet(zone_at, place_at, group_at):
        pl.semaphore_signal(
            barrier, inc=1, device_id=device(zone_at, place_at, group_at), device_id_type=MESH
        )

    pl.when(has_up)(lambda: greet(zone, place + 1, group))
    pl.when(has_down)(lambda: greet(zone, place - 1, group))
    pl.when(has_next)(lambda: greet(zone + 1, place, group))
    pl.when(has_left)(lambda: greet(zone - 1, place, group))
    for step in range(1, groups):
        greet(zone, place, lax.rem(group + step, groups))
    greeted = (
        has_up.astype(jnp.int32)
        + has_down.astype(jnp.int32)
        + has_next.astype(jnp.int32)
        + has_left.astype(jnp.int32)
        + (groups - 1)
    )
    pl.semaphore_wait(barrier, greeted)

    def hop_copy(way, hop, band, first):
        source = place - hop if way == 0 else place + hop
        target = place + 1 if way == 0 else place - 1
        return pltpu.make_async_remote_copy(
            src_ref=tiles.at[:, band] if first else planes.at[band, source],
            dst_ref=planes.at[band, source],
            send_sem=z_send.at[way, hop, band],
            recv_sem=z_recv.at[way, hop, band],
            device_id=device(zone, target, group),
            device_id_type=MESH,
        )

    def hop_arrival(way, hop, band):
        source = place - hop - 1 if way == 0 else place + hop + 1
        return pltpu.make_async_remote_copy(
            src_ref=planes.at[band, source],
            dst_ref=planes.at[band, source],
            send_sem=z_send.at[way, hop, band],
            recv_sem=z_recv.at[way, hop, band],
            device_id=device(zone, place - 1 if way == 0 else place + 1, group),
            device_id_type=MESH,
        )

    def seam_copy(source, band, own):
        return pltpu.make_async_remote_copy(
            src_ref=tiles.at[pl.ds(0, seam_count), band]
            if own
            else planes.at[band, source, pl.ds(0, seam_count)],
            dst_ref=seams.at[band, source],
            send_sem=y_send.at[source, band],
            recv_sem=y_recv.at[source, band],
            device_id=device(zone + 1, place, group),
            device_id_type=MESH,
        )

    def seam_arrival(source, band):
        return pltpu.make_async_remote_copy(
            src_ref=seams.at[band, source],
            dst_ref=seams.at[band, source],
            send_sem=y_send.at[source, band],
            recv_sem=y_recv.at[source, band],
            device_id=device(zone - 1, place, group),
            device_id_type=MESH,
        )

    def block_copy(step, band):
        target = lax.rem(group + step, groups)
        return pltpu.make_async_remote_copy(
            src_ref=out_v.at[band % 2, target],
            dst_ref=incoming.at[group, :, band],
            send_sem=x_send.at[step, band],
            recv_sem=x_recv.at[step, band],
            device_id=device(zone, place, target),
            device_id_type=MESH,
        )

    def block_arrival(step, band):
        sender = lax.rem(group + groups - step, groups)
        return pltpu.make_async_remote_copy(
            src_ref=out_v.at[band % 2, sender],
            dst_ref=incoming.at[sender, :, band],
            send_sem=x_send.at[step, band],
            recv_sem=x_recv.at[step, band],
            device_id=device(zone, place, sender),
            device_id_type=MESH,
        )

    def own_copy(band):
        return pltpu.make_async_copy(
            out_v.at[band % 2, group], incoming.at[group, :, band], own_sem.at[band % 2]
        )

    def sends_to(way, hop):
        if way == 0:
            return has_up & (place - hop >= 0)
        return has_down & (place + hop < line)

    def arrives_by(way, hop):
        if way == 0:
            return place - hop - 1 >= 0
        return place + hop + 1 < line

    def advance(step):
        for hop in range(line):
            band = step - lag * hop

            @pl.when((band >= 0) & (band < bands))
            def _():
                if hop == 0:

                    @pl.when(has_next)
                    def _():
                        seam_copy(place, band, True).start()

                for way in (0, 1):
                    if hop > 0:

                        @pl.when(arrives_by(way, hop - 1))
                        def _():
                            hop_arrival(way, hop - 1, band).wait_recv()

                    if hop < line - 1:

                        @pl.when(sends_to(way, hop))
                        def _():
                            hop_copy(way, hop, band, hop == 0).start()

                    if hop > 0:

                        @pl.when(arrives_by(way, hop - 1) & has_next)
                        def _():
                            source = place - hop if way == 0 else place + hop
                            seam_copy(source, band, False).start()

    def build(slot, carry):
        rows = lax.broadcasted_iota(jnp.int32, (height // 2, height), 0).astype(jnp.float32)
        cols = lax.broadcasted_iota(jnp.int32, (height // 2, height), 1).astype(jnp.float32)
        row_k[slot] = cubic_weight(cols - (2.0 * rows + shift_ref[slot, 0])).astype(jnp.bfloat16)
        rows = lax.broadcasted_iota(jnp.int32, (width, width // 2), 1).astype(jnp.float32)
        cols = lax.broadcasted_iota(jnp.int32, (width, width // 2), 0).astype(jnp.float32)
        col_k[slot] = cubic_weight(cols - (2.0 * rows + shift_ref[slot, 1])).astype(jnp.bfloat16)
        return carry

    def render(band, blended):
        def one(index, carry):
            for owner in range(groups):
                slot = owner * slots + index
                mixed = plane_v[prim_ref[slot]]
                if blended:
                    weight = weight_ref[slot]
                    other = seam_v[sec_ref[slot]]
                    mixed = (
                        (1.0 - weight) * mixed.astype(jnp.float32)
                        + weight * other.astype(jnp.float32)
                    ).astype(jnp.bfloat16)
                across = jnp.dot(mixed, col_k[slot], preferred_element_type=jnp.float32)
                result = jnp.dot(
                    row_k[slot],
                    across.astype(jnp.bfloat16),
                    preferred_element_type=jnp.float32,
                )
                out_v[band % 2, owner, index] = result.astype(jnp.bfloat16)
            return carry

        lax.fori_loop(0, slots, one, 0)

    def fetch(source, band, own):
        return pltpu.make_async_copy(
            tiles.at[:, band] if own else planes.at[band, source],
            plane_v.at[pl.ds(source * loc, loc)],
            local_sem.at[source],
        )

    def fetch_seam(source, band):
        return pltpu.make_async_copy(
            seams.at[band, source],
            seam_v.at[pl.ds(source * seam_count, seam_count)],
            local_sem.at[line + source],
        )

    def compute(band):
        for source in range(line):
            pl.when(place == source)(lambda: fetch(source, band, True).start())
            pl.when(place != source)(lambda: fetch(source, band, False).start())

        @pl.when(has_left)
        def _():
            for source in range(line):
                seam_arrival(source, band).wait_recv()
                fetch_seam(source, band).start()

        @pl.when(band >= 2)
        def _():
            for step in range(1, groups):
                block_copy(step, band - 2).wait_send()
            own_copy(band - 2).wait()

        for source in range(line):
            fetch(source, band, False).wait()

        @pl.when(has_left)
        def _():
            for source in range(line):
                fetch_seam(source, band).wait()
            render(band, True)

        @pl.when(jnp.logical_not(has_left))
        def _():
            render(band, False)

        for step in range(1, groups):
            block_copy(step, band).start()
        own_copy(band).start()

    head = lag * (line - 1)
    for step in range(lag):
        advance(step)
    lax.fori_loop(0, groups * slots, build, 0)

    def turn(step, carry):
        advance(step)
        band = step - head - 1

        @pl.when(band >= 0)
        def _():
            compute(band)

        return carry

    lax.fori_loop(lag, bands + head + 1, turn, 0)

    def settle(band, carry):
        for way in (0, 1):
            for hop in range(line - 1):

                @pl.when(sends_to(way, hop))
                def _():
                    hop_copy(way, hop, band, hop == 0).wait_send()

        @pl.when(has_next)
        def _():
            for source in range(line):
                pl.when(place == source)(lambda: seam_copy(source, band, True).wait_send())
                pl.when(place != source)(lambda: seam_copy(source, band, False).wait_send())

        @pl.when(band >= bands - 2)
        def _():
            for step in range(1, groups):
                block_copy(step, band).wait_send()
            own_copy(band).wait()

        for step in range(1, groups):
            block_arrival(step, band).wait_recv()
        return carry

    lax.fori_loop(0, bands, settle, 0)


def pick_kernel(pick_ref, block_ref, out_ref):
    out_ref[...] = block_ref[...]


def local(zones, tile_count, tiles, seam_list, source, offsets, fractions, blend):
    myself = lax.axis_index("tile")
    zone = lax.axis_index("zone")
    loc, bands, height, width = tiles.shape
    seam_count = seam_list.shape[0]
    line = line_length(tile_count)
    groups = tile_count // line
    place = myself // groups
    group = myself % groups
    per_owner = source.shape[0] // tile_count
    capacity = max(2, 2 * per_owner // tile_count)
    slots = min(per_owner, line * capacity)

    tile_ids = jnp.arange(loc, dtype=jnp.int32)
    list_ids = jnp.arange(seam_count, dtype=jnp.int32)

    def positions(lists):
        match = lists[..., None, :] == tile_ids[:, None]
        listed = jnp.any(match, axis=-1)
        at = jnp.sum(match * list_ids, axis=-1)
        free = jnp.logical_not(listed).astype(jnp.int32)
        below = (tile_ids[None, :] < tile_ids[:, None]).astype(jnp.int32)
        earlier = jnp.sum(free[..., None, :] * below, axis=-1)
        return jnp.where(listed, at, seam_count + earlier), listed

    mine, _ = positions(seam_list)
    order = jnp.sum(jnp.where(mine[None, :] == tile_ids[:, None], tile_ids[None, :], 0), axis=1)
    arranged = tiles[order]

    lists = lax.all_gather(seam_list, ("zone", "tile"), axis=0, tiled=True)
    lists = lists.reshape(zones, line, groups, seam_count)
    here = lax.dynamic_index_in_dim(lists[:, :, :, :], zone, 0, keepdims=False)
    here = lax.dynamic_index_in_dim(here, group, 1, keepdims=False)
    left = lax.dynamic_index_in_dim(lists, jnp.maximum(zone - 1, 0), 0, keepdims=False)
    left = lax.dynamic_index_in_dim(left, group, 1, keepdims=False)
    here_at, _ = positions(here)
    left_at, left_listed = positions(left)

    def rows_of(array):
        array = array.reshape((line, groups, per_owner) + array.shape[1:])
        return lax.dynamic_index_in_dim(array, place, 0, keepdims=False)

    wanted = rows_of(source)
    device = wanted // loc
    from_group = device % groups
    from_place = device // groups
    tile = wanted % loc
    ids = jnp.arange(per_owner, dtype=jnp.int32)
    same = from_group[:, :, None] == from_group[:, None, :]
    rank = jnp.sum((same & (ids[None, :] < ids[:, None])[None]).astype(jnp.int32), axis=2)
    entry = from_place * loc + tile
    primary = from_place * loc + here_at.reshape(-1)[entry]
    flagged = left_listed.reshape(-1)[entry] & (zone > 0)
    second = from_place * seam_count + jnp.where(
        left_listed.reshape(-1)[entry], left_at.reshape(-1)[entry], 0
    )
    weight = rows_of(blend) * flagged.astype(jnp.float32)
    shift = rows_of(offsets.astype(jnp.float32) + fractions)

    taken = (from_group == group)[:, None, :] & (
        rank[:, None, :] == jnp.arange(slots, dtype=jnp.int32)[None, :, None]
    )
    held = jnp.sum(taken.astype(jnp.int32) * ids, axis=2)
    flat = (jnp.arange(groups, dtype=jnp.int32)[:, None] * per_owner + held).reshape(-1)
    primary = primary.reshape(-1)[flat]
    second = second.reshape(-1)[flat]
    weight = weight.reshape(-1)[flat]
    shift = shift.reshape(-1, 2)[flat]
    picks = lax.dynamic_index_in_dim(from_group * slots + rank, group, 0, keepdims=False)

    half = (height // 2, width // 2)
    total = groups * slots
    any_space = pl.BlockSpec(memory_space=pl.ANY)
    smem = pl.BlockSpec(memory_space=pltpu.SMEM)
    kind = tiles.dtype
    _, _, incoming = pl.pallas_call(
        functools.partial(exchange_kernel, (zones, line, groups, slots)),
        out_shape=[
            jax.ShapeDtypeStruct((bands, line, loc, height, width), kind),
            jax.ShapeDtypeStruct((bands, line, seam_count, height, width), kind),
            jax.ShapeDtypeStruct((groups, slots, bands) + half, kind),
        ],
        in_specs=[smem] * 4 + [any_space],
        out_specs=[any_space] * 3,
        scratch_shapes=[
            pltpu.VMEM((total, height // 2, height), kind),
            pltpu.VMEM((total, width, width // 2), kind),
            pltpu.VMEM((line * loc, height, width), kind),
            pltpu.VMEM((line * seam_count, height, width), kind),
            pltpu.VMEM((2, groups, slots) + half, kind),
            pltpu.SemaphoreType.DMA((2, line - 1, bands)),
            pltpu.SemaphoreType.DMA((2, line - 1, bands)),
            pltpu.SemaphoreType.DMA((line, bands)),
            pltpu.SemaphoreType.DMA((line, bands)),
            pltpu.SemaphoreType.DMA((groups, bands)),
            pltpu.SemaphoreType.DMA((groups, bands)),
            pltpu.SemaphoreType.DMA((2 * line,)),
            pltpu.SemaphoreType.DMA((2,)),
        ],
        compiler_params=pltpu.CompilerParams(
            collective_id=0, has_side_effects=True, vmem_limit_bytes=40 * 1024 * 1024
        ),
    )(primary, second, weight, shift, arranged)

    incoming = incoming.reshape((total, bands) + half)
    return pl.pallas_call(
        pick_kernel,
        grid_spec=pltpu.PrefetchScalarGridSpec(
            num_scalar_prefetch=1,
            grid=(per_owner,),
            in_specs=[
                pl.BlockSpec((1, bands) + half, lambda block, pick: (pick[block], 0, 0, 0))
            ],
            out_specs=pl.BlockSpec((1, bands) + half, lambda block, pick: (block, 0, 0, 0)),
        ),
        out_shape=jax.ShapeDtypeStruct((per_owner, bands) + half, kind),
    )(picks, incoming)


def solution(mesh):
    in_specs = (
        P(("zone", "tile"), None, None, None),
        P(("zone", "tile")),
        P("zone"),
        P("zone", None),
        P("zone", None),
        P("zone"),
    )
    out_specs = P(("zone", "tile"), None, None, None)
    body = functools.partial(local, mesh.shape["zone"], mesh.shape["tile"])
    return jax.shard_map(body, mesh=mesh, in_specs=in_specs, out_specs=out_specs, check_vma=False)
```

```python
import functools
import math

import jax
import jax.numpy as jnp
from jax import lax
from jax.experimental import pallas as pl
from jax.experimental.pallas import tpu as pltpu
from jax.sharding import PartitionSpec as P

lag = 2
MESH = pl.DeviceIdType.MESH


def line_length(count):
    best = 1
    for length in range(1, count + 1):
        if count % length == 0 and length * length <= count:
            best = length
    return best


def cubic_weight(dist):
    mag = jnp.abs(dist)
    near = (1.5 * mag - 2.5) * mag * mag + 1.0
    far = ((-0.5 * mag + 2.5) * mag - 4.0) * mag + 2.0
    return jnp.where(mag <= 1.0, near, jnp.where(mag < 2.0, far, jnp.zeros_like(mag)))


def exchange_kernel(
    sizes,
    from_ref,
    tile_ref,
    blend_ref,
    shift_ref,
    order_ref,
    card_ref,
    tiles_hbm,
    planes,
    seams,
    incoming,
    row_k,
    col_k,
    plane_v,
    seam_v,
    out_v,
    raw_v,
    tiles,
    cards_v,
    cards,
    prim_ref,
    sec_ref,
    weight_ref,
    card_send,
    card_recv,
    z_send,
    z_recv,
    y_send,
    y_recv,
    x_send,
    x_recv,
    local_sem,
    own_sem,
):
    zones, line, groups, slots = sizes
    bands, loc, height, width = tiles.shape
    seam_count = seams.shape[2]
    zone = lax.axis_index("zone")
    myself = lax.axis_index("tile")
    place = myself // groups
    group = myself % groups

    def device(zone_at, place_at, group_at):
        return (zone_at, place_at * groups + group_at)

    has_up = place + 1 < line
    has_down = place >= 1
    has_next = zone + 1 < zones
    has_left = zone >= 1

    raw_copy = pltpu.make_async_copy(tiles_hbm, raw_v, own_sem.at[0])
    raw_copy.start()
    cards_v[...] = jnp.zeros_like(cards_v)
    cards_v[0, place] = card_ref[...]

    barrier = pltpu.get_barrier_semaphore()

    def greet(zone_at, place_at, group_at):
        pl.semaphore_signal(
            barrier, inc=1, device_id=device(zone_at, place_at, group_at), device_id_type=MESH
        )

    for other in range(line):
        pl.when(place != other)(lambda: greet(zone, other, group))
        pl.when(has_next)(lambda: greet(zone + 1, other, group))
        pl.when(has_left)(lambda: greet(zone - 1, other, group))
    for step in range(1, groups):
        greet(zone, place, lax.rem(group + step, groups))

    raw_copy.wait()

    def arrange(band, carry):
        for spot in range(loc):
            tiles[band, spot] = raw_v[order_ref[spot], band]
        return carry

    lax.fori_loop(0, bands, arrange, 0)
    greeted = (
        line * (has_next.astype(jnp.int32) + has_left.astype(jnp.int32)) + (line - 1) + (groups - 1)
    )
    pl.semaphore_wait(barrier, greeted)

    def card_copy(later, other):
        return pltpu.make_async_remote_copy(
            src_ref=card_ref,
            dst_ref=cards_v.at[later, place],
            send_sem=card_send.at[later, other],
            recv_sem=card_recv.at[later, place],
            device_id=device(zone + later, other, group),
            device_id_type=MESH,
        )

    def card_arrival(later, sender):
        return pltpu.make_async_remote_copy(
            src_ref=card_ref,
            dst_ref=cards_v.at[later, sender],
            send_sem=card_send.at[later, sender],
            recv_sem=card_recv.at[later, sender],
            device_id=device(zone - later, sender, group),
            device_id_type=MESH,
        )

    for other in range(line):
        pl.when(place != other)(lambda: card_copy(0, other).start())
        pl.when(has_next)(lambda: card_copy(1, other).start())

    def hop_copy(way, hop, band, first):
        source = place - hop if way == 0 else place + hop
        target = place + 1 if way == 0 else place - 1
        return pltpu.make_async_remote_copy(
            src_ref=tiles.at[band] if first else planes.at[band, source],
            dst_ref=planes.at[band, source],
            send_sem=z_send.at[way, hop, band],
            recv_sem=z_recv.at[way, hop, band],
            device_id=device(zone, target, group),
            device_id_type=MESH,
        )

    def hop_arrival(way, hop, band):
        source = place - hop - 1 if way == 0 else place + hop + 1
        return pltpu.make_async_remote_copy(
            src_ref=planes.at[band, source],
            dst_ref=planes.at[band, source],
            send_sem=z_send.at[way, hop, band],
            recv_sem=z_recv.at[way, hop, band],
            device_id=device(zone, place - 1 if way == 0 else place + 1, group),
            device_id_type=MESH,
        )

    def seam_copy(source, band, own):
        return pltpu.make_async_remote_copy(
            src_ref=tiles.at[band, pl.ds(0, seam_count)]
            if own
            else planes.at[band, source, pl.ds(0, seam_count)],
            dst_ref=seams.at[band, source],
            send_sem=y_send.at[source, band],
            recv_sem=y_recv.at[source, band],
            device_id=device(zone + 1, place, group),
            device_id_type=MESH,
        )

    def seam_arrival(source, band):
        return pltpu.make_async_remote_copy(
            src_ref=seams.at[band, source],
            dst_ref=seams.at[band, source],
            send_sem=y_send.at[source, band],
            recv_sem=y_recv.at[source, band],
            device_id=device(zone - 1, place, group),
            device_id_type=MESH,
        )

    def block_copy(step, band):
        target = lax.rem(group + step, groups)
        return pltpu.make_async_remote_copy(
            src_ref=out_v.at[band % 2, target],
            dst_ref=incoming.at[group, :, band],
            send_sem=x_send.at[step, band],
            recv_sem=x_recv.at[step, band],
            device_id=device(zone, place, target),
            device_id_type=MESH,
        )

    def block_arrival(step, band):
        sender = lax.rem(group + groups - step, groups)
        return pltpu.make_async_remote_copy(
            src_ref=out_v.at[band % 2, sender],
            dst_ref=incoming.at[sender, :, band],
            send_sem=x_send.at[step, band],
            recv_sem=x_recv.at[step, band],
            device_id=device(zone, place, sender),
            device_id_type=MESH,
        )

    def own_copy(band):
        return pltpu.make_async_copy(
            out_v.at[band % 2, group], incoming.at[group, :, band], own_sem.at[band % 2]
        )

    def sends_to(way, hop):
        if way == 0:
            return has_up & (place - hop >= 0)
        return has_down & (place + hop < line)

    def arrives_by(way, hop):
        if way == 0:
            return place - hop - 1 >= 0
        return place + hop + 1 < line

    def advance(step):
        for hop in range(line):
            band = step - lag * hop

            @pl.when((band >= 0) & (band < bands))
            def _():
                if hop == 0:

                    @pl.when(has_next)
                    def _():
                        seam_copy(place, band, True).start()

                for way in (0, 1):
                    if hop > 0:

                        @pl.when(arrives_by(way, hop - 1))
                        def _():
                            hop_arrival(way, hop - 1, band).wait_recv()

                    if hop < line - 1:

                        @pl.when(sends_to(way, hop))
                        def _():
                            hop_copy(way, hop, band, hop == 0).start()

                    if hop > 0:

                        @pl.when(arrives_by(way, hop - 1) & has_next)
                        def _():
                            source = place - hop if way == 0 else place + hop
                            seam_copy(source, band, False).start()

    def build(slot, carry):
        origin = from_ref[slot]
        tile = tile_ref[slot]
        listed, spot, below, flagged, second = 0, 0, 0, 0, 0
        for entry in range(seam_count):
            here = cards[0, origin, 0, entry]
            left = cards[1, origin, 0, entry]
            listed = listed + jnp.where(here == tile, 1, 0)
            spot = spot + jnp.where(here == tile, entry, 0)
            below = below + jnp.where(here < tile, 1, 0)
            flagged = flagged + jnp.where(left == tile, 1, 0)
            second = second + jnp.where(left == tile, entry, 0)
        spot = jnp.where(listed > 0, spot, seam_count + tile - below)
        prim_ref[slot] = origin * loc + spot
        sec_ref[slot] = origin * seam_count + second
        weight_ref[slot] = jnp.where(flagged > 0, blend_ref[slot], 0.0)
        rows = lax.broadcasted_iota(jnp.int32, (height // 2, height), 0).astype(jnp.float32)
        cols = lax.broadcasted_iota(jnp.int32, (height // 2, height), 1).astype(jnp.float32)
        row_k[slot] = cubic_weight(cols - (2.0 * rows + shift_ref[2 * slot])).astype(jnp.bfloat16)
        rows = lax.broadcasted_iota(jnp.int32, (width, width // 2), 1).astype(jnp.float32)
        cols = lax.broadcasted_iota(jnp.int32, (width, width // 2), 0).astype(jnp.float32)
        col_k[slot] = cubic_weight(cols - (2.0 * rows + shift_ref[2 * slot + 1])).astype(jnp.bfloat16)
        return carry

    together = math.gcd(slots, 4)

    def render(band, blended):
        def part(owner, index, carry):
            spots = [index * together + more for more in range(together)]
            mixed = []
            for spot in spots:
                slot = owner * slots + spot
                pixels = plane_v[prim_ref[slot]]
                if blended:
                    weight = weight_ref[slot]
                    other = seam_v[sec_ref[slot]]
                    pixels = (
                        (1.0 - weight) * pixels.astype(jnp.float32)
                        + weight * other.astype(jnp.float32)
                    ).astype(jnp.bfloat16)
                mixed.append(pixels)
            across = [
                jnp.dot(
                    pixels, col_k[owner * slots + spot], preferred_element_type=jnp.float32
                ).astype(jnp.bfloat16)
                for spot, pixels in zip(spots, mixed)
            ]
            results = [
                jnp.dot(row_k[owner * slots + spot], value, preferred_element_type=jnp.float32)
                for spot, value in zip(spots, across)
            ]
            for spot, result in zip(spots, results):
                out_v[band % 2, owner, spot] = result.astype(jnp.bfloat16)
            return carry

        def one_owner(step, carry):
            owner = lax.rem(group + step, groups)
            lax.fori_loop(0, slots // together, functools.partial(part, owner), 0)
            pl.when(step < groups)(lambda: block_copy(step, band).start())
            pl.when(step == groups)(lambda: own_copy(band).start())
            return carry

        lax.fori_loop(1, groups + 1, one_owner, 0)

    def fetch(source, band, own):
        return pltpu.make_async_copy(
            tiles.at[band] if own else planes.at[band, source],
            plane_v.at[pl.ds(source * loc, loc)],
            local_sem.at[source],
        )

    def fetch_seam(source, band):
        return pltpu.make_async_copy(
            seams.at[band, source],
            seam_v.at[pl.ds(source * seam_count, seam_count)],
            local_sem.at[line + source],
        )

    def compute(band):
        for source in range(line):
            pl.when(place == source)(lambda: fetch(source, band, True).start())
            pl.when(place != source)(lambda: fetch(source, band, False).start())

        @pl.when(has_left)
        def _():
            for source in range(line):
                seam_arrival(source, band).wait_recv()
                fetch_seam(source, band).start()

        @pl.when(band >= 2)
        def _():
            for step in range(1, groups):
                block_copy(step, band - 2).wait_send()
            own_copy(band - 2).wait()

        for source in range(line):
            fetch(source, band, False).wait()

        @pl.when(has_left)
        def _():
            for source in range(line):
                fetch_seam(source, band).wait()
            render(band, True)

        @pl.when(jnp.logical_not(has_left))
        def _():
            render(band, False)

    head = lag * (line - 1)
    for step in range(lag):
        advance(step)
    for sender in range(line):
        pl.when(place != sender)(lambda: card_arrival(0, sender).wait_recv())
        pl.when(has_left)(lambda: card_arrival(1, sender).wait_recv())
    cards_copy = pltpu.make_async_copy(cards_v, cards, own_sem.at[0])
    cards_copy.start()
    cards_copy.wait()
    lax.fori_loop(0, groups * slots, build, 0)

    def turn(step, carry):
        advance(step)
        band = step - head

        @pl.when(band >= 0)
        def _():
            compute(band)

        return carry

    lax.fori_loop(lag, bands + head, turn, 0)

    for other in range(line):
        pl.when(place != other)(lambda: card_copy(0, other).wait_send())
        pl.when(has_next)(lambda: card_copy(1, other).wait_send())

    def settle(band, carry):
        for way in (0, 1):
            for hop in range(line - 1):

                @pl.when(sends_to(way, hop))
                def _():
                    hop_copy(way, hop, band, hop == 0).wait_send()

        @pl.when(has_next)
        def _():
            for source in range(line):
                pl.when(place == source)(lambda: seam_copy(source, band, True).wait_send())
                pl.when(place != source)(lambda: seam_copy(source, band, False).wait_send())

        @pl.when(band >= bands - 2)
        def _():
            for step in range(1, groups):
                block_copy(step, band).wait_send()
            own_copy(band).wait()

        for step in range(1, groups):
            block_arrival(step, band).wait_recv()
        return carry

    lax.fori_loop(0, bands, settle, 0)


def table_kernel(
    sizes,
    seam_ref,
    source_ref,
    shift_ref,
    blend_ref,
    from_ref,
    tile_ref,
    weight_ref,
    moved_ref,
    pick_ref,
    order_ref,
    card_ref,
    counts,
):
    line, groups, slots, loc, per_owner = sizes
    seam_count = seam_ref.shape[0]
    myself = lax.axis_index("tile")
    place = myself // groups
    group = myself % groups

    def clear(slot, carry):
        from_ref[slot] = 0
        tile_ref[slot] = 0
        weight_ref[slot] = 0.0
        moved_ref[2 * slot] = 0.0
        moved_ref[2 * slot + 1] = 0.0
        return carry

    lax.fori_loop(0, groups * slots + 1, clear, 0)

    for owner in range(groups):

        def fill(index, count):
            block = (place * groups + owner) * per_owner + index
            value = source_ref[block]
            device = value // loc
            slot = owner * slots + count
            from_ref[slot] = device // groups
            tile_ref[slot] = value - device * loc
            weight_ref[slot] = blend_ref[block]
            moved_ref[2 * slot] = shift_ref[2 * block]
            moved_ref[2 * slot + 1] = shift_ref[2 * block + 1]
            return count + jnp.where(lax.rem(device, groups) == group, 1, 0)

        lax.fori_loop(0, per_owner, fill, 0)

    for sender in range(groups):
        counts[sender] = 0

    def choose(index, carry):
        sender = lax.rem(source_ref[myself * per_owner + index] // loc, groups)
        count = counts[sender]
        pick_ref[index] = sender * slots + count
        counts[sender] = count + 1
        return carry

    lax.fori_loop(0, per_owner, choose, 0)

    columns = lax.broadcasted_iota(jnp.int32, card_ref.shape, 1)
    card = jnp.zeros(card_ref.shape, jnp.int32)
    for entry in range(seam_count):
        card = jnp.where(columns == entry, seam_ref[entry], card)
    card_ref[...] = card
    for tile in range(loc):
        listed, spot, below = 0, 0, 0
        for entry in range(seam_count):
            listed = listed + jnp.where(seam_ref[entry] == tile, 1, 0)
            spot = spot + jnp.where(seam_ref[entry] == tile, entry, 0)
            below = below + jnp.where(seam_ref[entry] < tile, 1, 0)
        order_ref[jnp.where(listed > 0, spot, seam_count + tile - below)] = tile


def pick_kernel(pick_ref, incoming, out, sems):
    def copy(block):
        return pltpu.make_async_copy(incoming.at[pick_ref[block]], out.at[block], sems.at[block])

    def begin(block, carry):
        copy(block).start()
        return carry

    def finish(block, carry):
        copy(block).wait()
        return carry

    lax.fori_loop(0, out.shape[0], begin, 0)
    lax.fori_loop(0, out.shape[0], finish, 0)


def local(zones, tile_count, tiles, seam_list, source, offsets, fractions, blend):
    loc, bands, height, width = tiles.shape
    seam_count = seam_list.shape[0]
    line = line_length(tile_count)
    groups = tile_count // line
    per_owner = source.shape[0] // tile_count
    capacity = max(2, 2 * per_owner // tile_count)
    slots = min(per_owner, line * capacity)
    half = (height // 2, width // 2)
    total = groups * slots
    any_space = pl.BlockSpec(memory_space=pl.ANY)
    smem = pl.BlockSpec(memory_space=pltpu.SMEM)
    vmem = pl.BlockSpec(memory_space=pltpu.VMEM)
    kind = tiles.dtype

    shift = (offsets.astype(jnp.float32) + fractions).reshape(-1)
    came, tile, weight, moved, picks, order, card = pl.pallas_call(
        functools.partial(table_kernel, (line, groups, slots, loc, per_owner)),
        out_shape=[
            jax.ShapeDtypeStruct((total + 1,), jnp.int32),
            jax.ShapeDtypeStruct((total + 1,), jnp.int32),
            jax.ShapeDtypeStruct((total + 1,), jnp.float32),
            jax.ShapeDtypeStruct((2 * total + 2,), jnp.float32),
            jax.ShapeDtypeStruct((per_owner,), jnp.int32),
            jax.ShapeDtypeStruct((loc,), jnp.int32),
            jax.ShapeDtypeStruct((8, 128), jnp.int32),
        ],
        in_specs=[smem] * 4,
        out_specs=[smem] * 6 + [vmem],
        scratch_shapes=[pltpu.SMEM((groups,), jnp.int32)],
    )(seam_list, source, shift, blend)

    _, _, incoming = pl.pallas_call(
        functools.partial(exchange_kernel, (zones, line, groups, slots)),
        out_shape=[
            jax.ShapeDtypeStruct((bands, line, loc, height, width), kind),
            jax.ShapeDtypeStruct((bands, line, seam_count, height, width), kind),
            jax.ShapeDtypeStruct((groups, slots, bands) + half, kind),
        ],
        in_specs=[smem] * 5 + [vmem, any_space],
        out_specs=[any_space] * 3,
        scratch_shapes=[
            pltpu.VMEM((total, height // 2, height), kind),
            pltpu.VMEM((total, width, width // 2), kind),
            pltpu.VMEM((line * loc, height, width), kind),
            pltpu.VMEM((line * seam_count, height, width), kind),
            pltpu.VMEM((2, groups, slots) + half, kind),
            pltpu.VMEM((loc, bands, height, width), kind),
            pltpu.VMEM((bands, loc, height, width), kind),
            pltpu.VMEM((2, line, 8, 128), jnp.int32),
            pltpu.SMEM((2, line, 8, 128), jnp.int32),
            pltpu.SMEM((total,), jnp.int32),
            pltpu.SMEM((total,), jnp.int32),
            pltpu.SMEM((total,), jnp.float32),
            pltpu.SemaphoreType.DMA((2, line)),
            pltpu.SemaphoreType.DMA((2, line)),
            pltpu.SemaphoreType.DMA((2, line - 1, bands)),
            pltpu.SemaphoreType.DMA((2, line - 1, bands)),
            pltpu.SemaphoreType.DMA((line, bands)),
            pltpu.SemaphoreType.DMA((line, bands)),
            pltpu.SemaphoreType.DMA((groups, bands)),
            pltpu.SemaphoreType.DMA((groups, bands)),
            pltpu.SemaphoreType.DMA((2 * line,)),
            pltpu.SemaphoreType.DMA((2,)),
        ],
        compiler_params=pltpu.CompilerParams(
            collective_id=0, has_side_effects=True, vmem_limit_bytes=48 * 1024 * 1024
        ),
    )(came, tile, weight, moved, order, card, tiles)

    return pl.pallas_call(
        pick_kernel,
        in_specs=[smem, any_space],
        out_specs=any_space,
        out_shape=jax.ShapeDtypeStruct((per_owner, bands) + half, kind),
        scratch_shapes=[pltpu.SemaphoreType.DMA((per_owner,))],
    )(picks, incoming.reshape((total, bands) + half))


def solution(mesh):
    in_specs = (
        P(("zone", "tile"), None, None, None),
        P(("zone", "tile")),
        P("zone"),
        P("zone", None),
        P("zone", None),
        P("zone"),
    )
    out_specs = P(("zone", "tile"), None, None, None)
    body = functools.partial(local, mesh.shape["zone"], mesh.shape["tile"])
    return jax.shard_map(body, mesh=mesh, in_specs=in_specs, out_specs=out_specs, check_vma=False)
```

```python
import functools
import math

import jax
import jax.numpy as jnp
from jax import lax
from jax.experimental import pallas as pl
from jax.experimental.pallas import tpu as pltpu
from jax.sharding import PartitionSpec as P

pair = 2
lag = 2
MESH = pl.DeviceIdType.MESH


def line_length(count):
    best = 1
    for length in range(1, count + 1):
        if count % length == 0 and length * length <= count:
            best = length
    return best


def cubic_weight(dist):
    mag = jnp.abs(dist)
    near = (1.5 * mag - 2.5) * mag * mag + 1.0
    far = ((-0.5 * mag + 2.5) * mag - 4.0) * mag + 2.0
    return jnp.where(mag <= 1.0, near, jnp.where(mag < 2.0, far, jnp.zeros_like(mag)))


def exchange_kernel(
    sizes,
    from_ref,
    tile_ref,
    blend_ref,
    shift_ref,
    order_ref,
    card_ref,
    raw_v,
    planes,
    seams,
    incoming,
    row_k,
    col_k,
    plane_v,
    seam_v,
    out_v,
    tiles,
    cards_v,
    cards,
    prim_ref,
    sec_ref,
    weight_ref,
    card_send,
    card_recv,
    z_send,
    z_recv,
    y_send,
    y_recv,
    x_send,
    x_recv,
    local_sem,
    own_sem,
):
    zones, line, groups, slots = sizes
    bands, loc, height, width = tiles.shape
    seam_count = seams.shape[2]
    zone = lax.axis_index("zone")
    myself = lax.axis_index("tile")
    place = myself // groups
    group = myself % groups

    def device(zone_at, place_at, group_at):
        return (zone_at, place_at * groups + group_at)

    has_up = place + 1 < line
    has_down = place >= 1
    has_next = zone + 1 < zones
    has_left = zone >= 1

    cards_v[...] = jnp.zeros_like(cards_v)
    cards_v[0, place] = card_ref[...]

    barrier = pltpu.get_barrier_semaphore()

    def greet(zone_at, place_at, group_at):
        pl.semaphore_signal(
            barrier, inc=1, device_id=device(zone_at, place_at, group_at), device_id_type=MESH
        )

    for other in range(line):
        pl.when(place != other)(lambda: greet(zone, other, group))
        pl.when(has_next)(lambda: greet(zone + 1, other, group))
        pl.when(has_left)(lambda: greet(zone - 1, other, group))
    for step in range(1, groups):
        greet(zone, place, lax.rem(group + step, groups))


    def arrange(band, carry):
        for spot in range(loc):
            tiles[band, spot] = raw_v[order_ref[spot], band]
        return carry

    lax.fori_loop(0, bands, arrange, 0)
    greeted = (
        line * (has_next.astype(jnp.int32) + has_left.astype(jnp.int32)) + (line - 1) + (groups - 1)
    )
    pl.semaphore_wait(barrier, greeted)

    def card_copy(later, other):
        return pltpu.make_async_remote_copy(
            src_ref=card_ref,
            dst_ref=cards_v.at[later, place],
            send_sem=card_send.at[later, other],
            recv_sem=card_recv.at[later, place],
            device_id=device(zone + later, other, group),
            device_id_type=MESH,
        )

    def card_arrival(later, sender):
        return pltpu.make_async_remote_copy(
            src_ref=card_ref,
            dst_ref=cards_v.at[later, sender],
            send_sem=card_send.at[later, sender],
            recv_sem=card_recv.at[later, sender],
            device_id=device(zone - later, sender, group),
            device_id_type=MESH,
        )

    for other in range(line):
        pl.when(place != other)(lambda: card_copy(0, other).start())
        pl.when(has_next)(lambda: card_copy(1, other).start())

    def hop_copy(way, hop, band, first):
        source = place - hop if way == 0 else place + hop
        target = place + 1 if way == 0 else place - 1
        return pltpu.make_async_remote_copy(
            src_ref=tiles.at[band] if first else planes.at[band, source],
            dst_ref=planes.at[band, source],
            send_sem=z_send.at[way, hop, band],
            recv_sem=z_recv.at[way, hop, band],
            device_id=device(zone, target, group),
            device_id_type=MESH,
        )

    def hop_arrival(way, hop, band):
        source = place - hop - 1 if way == 0 else place + hop + 1
        return pltpu.make_async_remote_copy(
            src_ref=planes.at[band, source],
            dst_ref=planes.at[band, source],
            send_sem=z_send.at[way, hop, band],
            recv_sem=z_recv.at[way, hop, band],
            device_id=device(zone, place - 1 if way == 0 else place + 1, group),
            device_id_type=MESH,
        )

    def seam_copy(source, band, own):
        return pltpu.make_async_remote_copy(
            src_ref=tiles.at[band, pl.ds(0, seam_count)]
            if own
            else planes.at[band, source, pl.ds(0, seam_count)],
            dst_ref=seams.at[band, source],
            send_sem=y_send.at[source, band],
            recv_sem=y_recv.at[source, band],
            device_id=device(zone + 1, place, group),
            device_id_type=MESH,
        )

    def seam_arrival(source, band):
        return pltpu.make_async_remote_copy(
            src_ref=seams.at[band, source],
            dst_ref=seams.at[band, source],
            send_sem=y_send.at[source, band],
            recv_sem=y_recv.at[source, band],
            device_id=device(zone - 1, place, group),
            device_id_type=MESH,
        )

    chunks = incoming.shape[2] // pair
    spare = incoming.shape[2] - bands

    def landing(owner, chunk):
        return incoming.at[owner, :, pl.ds(chunk * pair, pair)]

    def block_copy(step, band):
        target = lax.rem(group + step, groups)
        return pltpu.make_async_remote_copy(
            src_ref=out_v.at[band % 2, target],
            dst_ref=landing(group, band),
            send_sem=x_send.at[step, band],
            recv_sem=x_recv.at[step, band],
            device_id=device(zone, place, target),
            device_id_type=MESH,
        )

    def block_arrival(step, band):
        sender = lax.rem(group + groups - step, groups)
        return pltpu.make_async_remote_copy(
            src_ref=out_v.at[band % 2, sender],
            dst_ref=landing(sender, band),
            send_sem=x_send.at[step, band],
            recv_sem=x_recv.at[step, band],
            device_id=device(zone, place, sender),
            device_id_type=MESH,
        )

    def own_copy(band):
        return pltpu.make_async_copy(
            out_v.at[band % 2, group], landing(group, band), own_sem.at[band % 2]
        )

    def sends_to(way, hop):
        if way == 0:
            return has_up & (place - hop >= 0)
        return has_down & (place + hop < line)

    def arrives_by(way, hop):
        if way == 0:
            return place - hop - 1 >= 0
        return place + hop + 1 < line

    def advance(step):
        for hop in range(line):
            band = step - lag * hop

            @pl.when((band >= 0) & (band < bands))
            def _():
                if hop == 0:

                    @pl.when(has_next)
                    def _():
                        seam_copy(place, band, True).start()

                for way in (0, 1):
                    if hop > 0:

                        @pl.when(arrives_by(way, hop - 1))
                        def _():
                            hop_arrival(way, hop - 1, band).wait_recv()

                    if hop < line - 1:

                        @pl.when(sends_to(way, hop))
                        def _():
                            hop_copy(way, hop, band, hop == 0).start()

                    if hop > 0:

                        @pl.when(arrives_by(way, hop - 1) & has_next)
                        def _():
                            source = place - hop if way == 0 else place + hop
                            seam_copy(source, band, False).start()

    def build(slot, carry):
        origin = from_ref[slot]
        tile = tile_ref[slot]
        listed, spot, below, flagged, second = 0, 0, 0, 0, 0
        for entry in range(seam_count):
            here = cards[0, origin, 0, entry]
            left = cards[1, origin, 0, entry]
            listed = listed + jnp.where(here == tile, 1, 0)
            spot = spot + jnp.where(here == tile, entry, 0)
            below = below + jnp.where(here < tile, 1, 0)
            flagged = flagged + jnp.where(left == tile, 1, 0)
            second = second + jnp.where(left == tile, entry, 0)
        spot = jnp.where(listed > 0, spot, seam_count + tile - below)
        prim_ref[slot] = origin * loc + spot
        sec_ref[slot] = origin * seam_count + second
        weight_ref[slot] = jnp.where(flagged > 0, blend_ref[slot], 0.0)
        rows = lax.broadcasted_iota(jnp.int32, (height // 2, height), 0).astype(jnp.float32)
        cols = lax.broadcasted_iota(jnp.int32, (height // 2, height), 1).astype(jnp.float32)
        row_k[slot] = cubic_weight(cols - (2.0 * rows + shift_ref[2 * slot])).astype(jnp.bfloat16)
        rows = lax.broadcasted_iota(jnp.int32, (width, width // 2), 1).astype(jnp.float32)
        cols = lax.broadcasted_iota(jnp.int32, (width, width // 2), 0).astype(jnp.float32)
        col_k[slot] = cubic_weight(cols - (2.0 * rows + shift_ref[2 * slot + 1])).astype(jnp.bfloat16)
        return carry

    together = math.gcd(slots, 2)

    def render(band, blended):
        def part(owner, index, carry):
            spots = [index * together + more for more in range(together)]
            mixed = []
            for spot in spots:
                slot = owner * slots + spot
                parts = []
                for half in range(pair):
                    pixels = plane_v[half, prim_ref[slot]]
                    if blended:
                        weight = weight_ref[slot]
                        other = seam_v[half, sec_ref[slot]]
                        pixels = (
                            (1.0 - weight) * pixels.astype(jnp.float32)
                            + weight * other.astype(jnp.float32)
                        ).astype(jnp.bfloat16)
                    parts.append(pixels)
                mixed.append(jnp.concatenate(parts, axis=0))
            across = [
                jnp.dot(
                    pixels, col_k[owner * slots + spot], preferred_element_type=jnp.float32
                ).astype(jnp.bfloat16)
                for spot, pixels in zip(spots, mixed)
            ]
            results = [
                jnp.dot(
                    row_k[owner * slots + spot],
                    jnp.concatenate(
                        [value[half * height : (half + 1) * height] for half in range(pair)],
                        axis=1,
                    ),
                    preferred_element_type=jnp.float32,
                ).astype(jnp.bfloat16)
                for spot, value in zip(spots, across)
            ]
            for spot, result in zip(spots, results):
                for half in range(pair):
                    out_v[band % 2, owner, spot, half] = result[
                        :, half * (width // 2) : (half + 1) * (width // 2)
                    ]
            return carry

        def one_owner(step, carry):
            owner = lax.rem(group + step, groups)
            lax.fori_loop(0, slots // together, functools.partial(part, owner), 0)
            pl.when(step < groups)(lambda: block_copy(step, band).start())
            pl.when(step == groups)(lambda: own_copy(band).start())
            return carry

        lax.fori_loop(1, groups + 1, one_owner, 0)

    def fetch(source, band, half, own):
        return pltpu.make_async_copy(
            tiles.at[band] if own else planes.at[band, source],
            plane_v.at[half, pl.ds(source * loc, loc)],
            local_sem.at[half, source],
        )

    def fetch_seam(source, band, half):
        return pltpu.make_async_copy(
            seams.at[band, source],
            seam_v.at[half, pl.ds(source * seam_count, seam_count)],
            local_sem.at[half, line + source],
        )

    def compute(chunk):
        real = [chunk * pair - spare + half for half in range(pair)]
        used = [jnp.maximum(band, 0) for band in real]
        for half in range(pair):
            for source in range(line):
                pl.when(place == source)(lambda: fetch(source, used[half], half, True).start())
                pl.when(place != source)(lambda: fetch(source, used[half], half, False).start())

        @pl.when(has_left)
        def _():
            for half in range(pair):

                @pl.when(real[half] >= 0)
                def _():
                    for source in range(line):
                        seam_arrival(source, used[half]).wait_recv()

            for half in range(pair):
                for source in range(line):
                    fetch_seam(source, used[half], half).start()

        @pl.when(chunk >= 2)
        def _():
            for step in range(1, groups):
                block_copy(step, chunk - 2).wait_send()
            own_copy(chunk - 2).wait()

        for half in range(pair):
            for source in range(line):
                fetch(source, used[half], half, False).wait()

        @pl.when(has_left)
        def _():
            for half in range(pair):
                for source in range(line):
                    fetch_seam(source, used[half], half).wait()
            render(chunk, True)

        @pl.when(jnp.logical_not(has_left))
        def _():
            render(chunk, False)

    head = lag * (line - 1)
    for step in range(lag):
        advance(step)
    for sender in range(line):
        pl.when(place != sender)(lambda: card_arrival(0, sender).wait_recv())
        pl.when(has_left)(lambda: card_arrival(1, sender).wait_recv())
    cards_copy = pltpu.make_async_copy(cards_v, cards, own_sem.at[0])
    cards_copy.start()
    cards_copy.wait()
    lax.fori_loop(0, groups * slots, build, 0)

    def turn(step, carry):
        advance(step)
        done = step - head + 1 + spare

        @pl.when((step >= head) & (done % pair == 0))
        def _():
            compute(done // pair - 1)

        return carry

    lax.fori_loop(lag, bands + head, turn, 0)

    for other in range(line):
        pl.when(place != other)(lambda: card_copy(0, other).wait_send())
        pl.when(has_next)(lambda: card_copy(1, other).wait_send())

    def settle(band, carry):
        for way in (0, 1):
            for hop in range(line - 1):

                @pl.when(sends_to(way, hop))
                def _():
                    hop_copy(way, hop, band, hop == 0).wait_send()

        @pl.when(has_next)
        def _():
            for source in range(line):
                pl.when(place == source)(lambda: seam_copy(source, band, True).wait_send())
                pl.when(place != source)(lambda: seam_copy(source, band, False).wait_send())

        return carry

    lax.fori_loop(0, bands, settle, 0)

    def gather_in(chunk, carry):
        @pl.when(chunk >= chunks - 2)
        def _():
            for step in range(1, groups):
                block_copy(step, chunk).wait_send()
            own_copy(chunk).wait()

        for step in range(1, groups):
            block_arrival(step, chunk).wait_recv()
        return carry

    lax.fori_loop(0, chunks, gather_in, 0)


def table_kernel(
    sizes,
    seam_ref,
    source_ref,
    shift_ref,
    blend_ref,
    from_ref,
    tile_ref,
    weight_ref,
    moved_ref,
    pick_ref,
    order_ref,
    card_ref,
    counts,
):
    line, groups, slots, loc, per_owner = sizes
    seam_count = seam_ref.shape[0]
    myself = lax.axis_index("tile")
    place = myself // groups
    group = myself % groups

    def clear(slot, carry):
        from_ref[slot] = 0
        tile_ref[slot] = 0
        weight_ref[slot] = 0.0
        moved_ref[2 * slot] = 0.0
        moved_ref[2 * slot + 1] = 0.0
        return carry

    lax.fori_loop(0, groups * slots + 1, clear, 0)

    for owner in range(groups):

        def fill(index, count):
            block = (place * groups + owner) * per_owner + index
            value = source_ref[block]
            device = value // loc
            slot = owner * slots + count
            from_ref[slot] = device // groups
            tile_ref[slot] = value - device * loc
            weight_ref[slot] = blend_ref[block]
            moved_ref[2 * slot] = shift_ref[2 * block]
            moved_ref[2 * slot + 1] = shift_ref[2 * block + 1]
            return count + jnp.where(lax.rem(device, groups) == group, 1, 0)

        lax.fori_loop(0, per_owner, fill, 0)

    for sender in range(groups):
        counts[sender] = 0

    def choose(index, carry):
        sender = lax.rem(source_ref[myself * per_owner + index] // loc, groups)
        count = counts[sender]
        pick_ref[index] = sender * slots + count
        counts[sender] = count + 1
        return carry

    lax.fori_loop(0, per_owner, choose, 0)

    columns = lax.broadcasted_iota(jnp.int32, card_ref.shape, 1)
    card = jnp.zeros(card_ref.shape, jnp.int32)
    for entry in range(seam_count):
        card = jnp.where(columns == entry, seam_ref[entry], card)
    card_ref[...] = card
    for tile in range(loc):
        listed, spot, below = 0, 0, 0
        for entry in range(seam_count):
            listed = listed + jnp.where(seam_ref[entry] == tile, 1, 0)
            spot = spot + jnp.where(seam_ref[entry] == tile, entry, 0)
            below = below + jnp.where(seam_ref[entry] < tile, 1, 0)
        order_ref[jnp.where(listed > 0, spot, seam_count + tile - below)] = tile


def pick_kernel(pick_ref, incoming, out, held, in_sems, out_sems):
    spare = incoming.shape[1] - out.shape[1]

    def copy_in(block):
        return pltpu.make_async_copy(
            incoming.at[pick_ref[block], pl.ds(spare, out.shape[1])],
            held.at[block],
            in_sems.at[block],
        )

    def copy_out(block):
        return pltpu.make_async_copy(held.at[block], out.at[block], out_sems.at[block])

    def begin(block, carry):
        copy_in(block).start()
        return carry

    def relay(block, carry):
        copy_in(block).wait()
        copy_out(block).start()
        return carry

    def finish(block, carry):
        copy_out(block).wait()
        return carry

    lax.fori_loop(0, out.shape[0], begin, 0)
    lax.fori_loop(0, out.shape[0], relay, 0)
    lax.fori_loop(0, out.shape[0], finish, 0)


def local(zones, tile_count, tiles, seam_list, source, offsets, fractions, blend):
    loc, bands, height, width = tiles.shape
    seam_count = seam_list.shape[0]
    line = line_length(tile_count)
    groups = tile_count // line
    per_owner = source.shape[0] // tile_count
    capacity = max(2, 2 * per_owner // tile_count)
    slots = min(per_owner, line * capacity)
    half = (height // 2, width // 2)
    total = groups * slots
    padded = -(-bands // pair) * pair
    any_space = pl.BlockSpec(memory_space=pl.ANY)
    smem = pl.BlockSpec(memory_space=pltpu.SMEM)
    vmem = pl.BlockSpec(memory_space=pltpu.VMEM)
    kind = tiles.dtype

    shift = (offsets.astype(jnp.float32) + fractions).reshape(-1)
    came, tile, weight, moved, picks, order, card = pl.pallas_call(
        functools.partial(table_kernel, (line, groups, slots, loc, per_owner)),
        out_shape=[
            jax.ShapeDtypeStruct((total + 1,), jnp.int32),
            jax.ShapeDtypeStruct((total + 1,), jnp.int32),
            jax.ShapeDtypeStruct((total + 1,), jnp.float32),
            jax.ShapeDtypeStruct((2 * total + 2,), jnp.float32),
            jax.ShapeDtypeStruct((per_owner,), jnp.int32),
            jax.ShapeDtypeStruct((loc,), jnp.int32),
            jax.ShapeDtypeStruct((8, 128), jnp.int32),
        ],
        in_specs=[smem] * 4,
        out_specs=[smem] * 6 + [vmem],
        scratch_shapes=[pltpu.SMEM((groups,), jnp.int32)],
    )(seam_list, source, shift, blend)

    _, _, incoming = pl.pallas_call(
        functools.partial(exchange_kernel, (zones, line, groups, slots)),
        out_shape=[
            jax.ShapeDtypeStruct((bands, line, loc, height, width), kind),
            jax.ShapeDtypeStruct((bands, line, seam_count, height, width), kind),
            jax.ShapeDtypeStruct((groups, slots, padded) + half, kind),
        ],
        in_specs=[smem] * 5 + [vmem, vmem],
        out_specs=[any_space] * 3,
        scratch_shapes=[
            pltpu.VMEM((total, height // 2, height), kind),
            pltpu.VMEM((total, width, width // 2), kind),
            pltpu.VMEM((pair, line * loc, height, width), kind),
            pltpu.VMEM((pair, line * seam_count, height, width), kind),
            pltpu.VMEM((2, groups, slots, pair) + half, kind),
            pltpu.VMEM((bands, loc, height, width), kind),
            pltpu.VMEM((2, line, 8, 128), jnp.int32),
            pltpu.SMEM((2, line, 8, 128), jnp.int32),
            pltpu.SMEM((total,), jnp.int32),
            pltpu.SMEM((total,), jnp.int32),
            pltpu.SMEM((total,), jnp.float32),
            pltpu.SemaphoreType.DMA((2, line)),
            pltpu.SemaphoreType.DMA((2, line)),
            pltpu.SemaphoreType.DMA((2, line - 1, bands)),
            pltpu.SemaphoreType.DMA((2, line - 1, bands)),
            pltpu.SemaphoreType.DMA((line, bands)),
            pltpu.SemaphoreType.DMA((line, bands)),
            pltpu.SemaphoreType.DMA((groups, padded // pair)),
            pltpu.SemaphoreType.DMA((groups, padded // pair)),
            pltpu.SemaphoreType.DMA((pair, 2 * line)),
            pltpu.SemaphoreType.DMA((2,)),
        ],
        compiler_params=pltpu.CompilerParams(
            collective_id=0, has_side_effects=True, vmem_limit_bytes=52 * 1024 * 1024
        ),
    )(came, tile, weight, moved, order, card, tiles)

    return pl.pallas_call(
        pick_kernel,
        in_specs=[smem, any_space],
        out_specs=any_space,
        out_shape=jax.ShapeDtypeStruct((per_owner, bands) + half, kind),
        scratch_shapes=[
            pltpu.VMEM((per_owner, bands) + half, kind),
            pltpu.SemaphoreType.DMA((per_owner,)),
            pltpu.SemaphoreType.DMA((per_owner,)),
        ],
        compiler_params=pltpu.CompilerParams(vmem_limit_bytes=32 * 1024 * 1024),
    )(picks, incoming.reshape((total, padded) + half))


def solution(mesh):
    in_specs = (
        P(("zone", "tile"), None, None, None),
        P(("zone", "tile")),
        P("zone"),
        P("zone", None),
        P("zone", None),
        P("zone"),
    )
    out_specs = P(("zone", "tile"), None, None, None)
    body = functools.partial(local, mesh.shape["zone"], mesh.shape["tile"])
    return jax.shard_map(body, mesh=mesh, in_specs=in_specs, out_specs=out_specs, check_vma=False)
```

```python
import functools
import math

import jax
import jax.numpy as jnp
from jax import lax
from jax.experimental import pallas as pl
from jax.experimental.pallas import tpu as pltpu
from jax.sharding import PartitionSpec as P

pair = 1
lead = 1
MESH = pl.DeviceIdType.MESH


def line_length(count):
    best = 1
    for length in range(1, count + 1):
        if count % length == 0 and length * length <= count:
            best = length
    return best


def cubic_weight(dist):
    mag = jnp.abs(dist)
    near = (1.5 * mag - 2.5) * mag * mag + 1.0
    far = ((-0.5 * mag + 2.5) * mag - 4.0) * mag + 2.0
    return jnp.where(mag <= 1.0, near, jnp.where(mag < 2.0, far, jnp.zeros_like(mag)))


def exchange_kernel(
    sizes,
    from_ref,
    tile_ref,
    blend_ref,
    shift_ref,
    order_ref,
    card_ref,
    raw_v,
    planes,
    seams,
    incoming,
    row_k,
    col_k,
    plane_v,
    seam_v,
    out_v,
    tiles,
    cards_v,
    cards,
    prim_ref,
    sec_ref,
    weight_ref,
    card_send,
    card_recv,
    z_send,
    z_recv,
    y_send,
    y_recv,
    x_send,
    x_recv,
    local_sem,
    own_sem,
):
    zones, line, groups, slots = sizes
    bands, loc, height, width = tiles.shape
    seam_count = seams.shape[2]
    zone = lax.axis_index("zone")
    myself = lax.axis_index("tile")
    place = myself // groups
    group = myself % groups

    def device(zone_at, place_at, group_at):
        return (zone_at, place_at * groups + group_at)

    has_up = place + 1 < line
    has_down = place >= 1
    has_next = zone + 1 < zones
    has_left = zone >= 1

    cards_v[...] = jnp.zeros_like(cards_v)
    cards_v[0, place] = card_ref[...]

    barrier = pltpu.get_barrier_semaphore()

    def greet(zone_at, place_at, group_at):
        pl.semaphore_signal(
            barrier, inc=1, device_id=device(zone_at, place_at, group_at), device_id_type=MESH
        )

    for other in range(line):
        pl.when(place != other)(lambda: greet(zone, other, group))
        pl.when(has_next)(lambda: greet(zone + 1, other, group))
        pl.when(has_left)(lambda: greet(zone - 1, other, group))
    for step in range(1, groups):
        greet(zone, place, lax.rem(group + step, groups))


    def arrange(band, carry):
        for spot in range(loc):
            tiles[band, spot] = raw_v[order_ref[spot], band]
        return carry

    lax.fori_loop(0, bands, arrange, 0)
    greeted = (
        line * (has_next.astype(jnp.int32) + has_left.astype(jnp.int32)) + (line - 1) + (groups - 1)
    )
    pl.semaphore_wait(barrier, greeted)

    def card_copy(later, other):
        return pltpu.make_async_remote_copy(
            src_ref=card_ref,
            dst_ref=cards_v.at[later, place],
            send_sem=card_send.at[later, other],
            recv_sem=card_recv.at[later, place],
            device_id=device(zone + later, other, group),
            device_id_type=MESH,
        )

    def card_arrival(later, sender):
        return pltpu.make_async_remote_copy(
            src_ref=card_ref,
            dst_ref=cards_v.at[later, sender],
            send_sem=card_send.at[later, sender],
            recv_sem=card_recv.at[later, sender],
            device_id=device(zone - later, sender, group),
            device_id_type=MESH,
        )

    for other in range(line):
        pl.when(place != other)(lambda: card_copy(0, other).start())
        pl.when(has_next)(lambda: card_copy(1, other).start())

    def hop_copy(way, hop, band, first):
        source = place - hop if way == 0 else place + hop
        target = place + 1 if way == 0 else place - 1
        return pltpu.make_async_remote_copy(
            src_ref=tiles.at[band] if first else planes.at[band, source],
            dst_ref=planes.at[band, source],
            send_sem=z_send.at[way, hop, band],
            recv_sem=z_recv.at[way, hop, band],
            device_id=device(zone, target, group),
            device_id_type=MESH,
        )

    def hop_arrival(way, hop, band):
        source = place - hop - 1 if way == 0 else place + hop + 1
        return pltpu.make_async_remote_copy(
            src_ref=planes.at[band, source],
            dst_ref=planes.at[band, source],
            send_sem=z_send.at[way, hop, band],
            recv_sem=z_recv.at[way, hop, band],
            device_id=device(zone, place - 1 if way == 0 else place + 1, group),
            device_id_type=MESH,
        )

    def seam_copy(source, band, own):
        return pltpu.make_async_remote_copy(
            src_ref=tiles.at[band, pl.ds(0, seam_count)]
            if own
            else planes.at[band, source, pl.ds(0, seam_count)],
            dst_ref=seams.at[band, source],
            send_sem=y_send.at[source, band],
            recv_sem=y_recv.at[source, band],
            device_id=device(zone + 1, place, group),
            device_id_type=MESH,
        )

    def seam_arrival(source, band):
        return pltpu.make_async_remote_copy(
            src_ref=seams.at[band, source],
            dst_ref=seams.at[band, source],
            send_sem=y_send.at[source, band],
            recv_sem=y_recv.at[source, band],
            device_id=device(zone - 1, place, group),
            device_id_type=MESH,
        )

    chunks = incoming.shape[2] // pair
    spare = incoming.shape[2] - bands

    def landing(owner, chunk):
        return incoming.at[owner, :, pl.ds(chunk * pair, pair)]

    def block_copy(step, band):
        target = lax.rem(group + step, groups)
        return pltpu.make_async_remote_copy(
            src_ref=out_v.at[band % 2, target],
            dst_ref=landing(group, band),
            send_sem=x_send.at[step, band],
            recv_sem=x_recv.at[step, band],
            device_id=device(zone, place, target),
            device_id_type=MESH,
        )

    def block_arrival(step, band):
        sender = lax.rem(group + groups - step, groups)
        return pltpu.make_async_remote_copy(
            src_ref=out_v.at[band % 2, sender],
            dst_ref=landing(sender, band),
            send_sem=x_send.at[step, band],
            recv_sem=x_recv.at[step, band],
            device_id=device(zone, place, sender),
            device_id_type=MESH,
        )

    def own_copy(band):
        return pltpu.make_async_copy(
            out_v.at[band % 2, group], landing(group, band), own_sem.at[band % 2]
        )

    def sends_to(way, hop):
        if way == 0:
            return has_up & (place - hop >= 0)
        return has_down & (place + hop < line)

    def arrives_by(way, hop):
        if way == 0:
            return place - hop - 1 >= 0
        return place + hop + 1 < line

    def advance(step):
        for hop in reversed(range(line)):
            band = step - hop - (lead if hop > 0 else 0)

            @pl.when((band >= 0) & (band < bands))
            def _():
                if hop == 0:

                    @pl.when(has_next)
                    def _():
                        seam_copy(place, band, True).start()

                for way in (0, 1):
                    if hop > 0:

                        @pl.when(arrives_by(way, hop - 1))
                        def _():
                            hop_arrival(way, hop - 1, band).wait_recv()

                    if hop < line - 1:

                        @pl.when(sends_to(way, hop))
                        def _():
                            hop_copy(way, hop, band, hop == 0).start()

                    if hop > 0:

                        @pl.when(arrives_by(way, hop - 1) & has_next)
                        def _():
                            source = place - hop if way == 0 else place + hop
                            seam_copy(source, band, False).start()

    def build(slot, carry):
        origin = from_ref[slot]
        tile = tile_ref[slot]
        listed, spot, below, flagged, second = 0, 0, 0, 0, 0
        for entry in range(seam_count):
            here = cards[0, origin, 0, entry]
            left = cards[1, origin, 0, entry]
            listed = listed + jnp.where(here == tile, 1, 0)
            spot = spot + jnp.where(here == tile, entry, 0)
            below = below + jnp.where(here < tile, 1, 0)
            flagged = flagged + jnp.where(left == tile, 1, 0)
            second = second + jnp.where(left == tile, entry, 0)
        spot = jnp.where(listed > 0, spot, seam_count + tile - below)
        prim_ref[slot] = origin * loc + spot
        sec_ref[slot] = origin * seam_count + second
        weight_ref[slot] = jnp.where(flagged > 0, blend_ref[slot], 0.0)
        rows = lax.broadcasted_iota(jnp.int32, (height // 2, height), 0).astype(jnp.float32)
        cols = lax.broadcasted_iota(jnp.int32, (height // 2, height), 1).astype(jnp.float32)
        row_k[slot] = cubic_weight(cols - (2.0 * rows + shift_ref[2 * slot])).astype(jnp.bfloat16)
        rows = lax.broadcasted_iota(jnp.int32, (width, width // 2), 1).astype(jnp.float32)
        cols = lax.broadcasted_iota(jnp.int32, (width, width // 2), 0).astype(jnp.float32)
        col_k[slot] = cubic_weight(cols - (2.0 * rows + shift_ref[2 * slot + 1])).astype(jnp.bfloat16)
        return carry

    together = math.gcd(slots, 4)

    def render(band, blended):
        def part(owner, index, carry):
            spots = [index * together + more for more in range(together)]
            mixed = []
            for spot in spots:
                slot = owner * slots + spot
                parts = []
                for half in range(pair):
                    pixels = plane_v[half, prim_ref[slot]]
                    if blended:
                        weight = weight_ref[slot]
                        other = seam_v[half, sec_ref[slot]]
                        pixels = (
                            (1.0 - weight) * pixels.astype(jnp.float32)
                            + weight * other.astype(jnp.float32)
                        ).astype(jnp.bfloat16)
                    parts.append(pixels)
                mixed.append(jnp.concatenate(parts, axis=0))
            across = [
                jnp.dot(
                    pixels, col_k[owner * slots + spot], preferred_element_type=jnp.float32
                ).astype(jnp.bfloat16)
                for spot, pixels in zip(spots, mixed)
            ]
            results = [
                jnp.dot(
                    row_k[owner * slots + spot],
                    jnp.concatenate(
                        [value[half * height : (half + 1) * height] for half in range(pair)],
                        axis=1,
                    ),
                    preferred_element_type=jnp.float32,
                ).astype(jnp.bfloat16)
                for spot, value in zip(spots, across)
            ]
            for spot, result in zip(spots, results):
                for half in range(pair):
                    out_v[band % 2, owner, spot, half] = result[
                        :, half * (width // 2) : (half + 1) * (width // 2)
                    ]
            return carry

        def one_owner(step, carry):
            owner = lax.rem(group + step, groups)
            lax.fori_loop(0, slots // together, functools.partial(part, owner), 0)
            pl.when(step < groups)(lambda: block_copy(step, band).start())
            pl.when(step == groups)(lambda: own_copy(band).start())
            return carry

        lax.fori_loop(1, groups + 1, one_owner, 0)

    def fetch(source, band, half, own):
        return pltpu.make_async_copy(
            tiles.at[band] if own else planes.at[band, source],
            plane_v.at[half, pl.ds(source * loc, loc)],
            local_sem.at[half, source],
        )

    def fetch_seam(source, band, half):
        return pltpu.make_async_copy(
            seams.at[band, source],
            seam_v.at[half, pl.ds(source * seam_count, seam_count)],
            local_sem.at[half, line + source],
        )

    def compute(chunk):
        real = [chunk * pair - spare + half for half in range(pair)]
        used = [jnp.maximum(band, 0) for band in real]
        for half in range(pair):
            for source in range(line):
                pl.when(place == source)(lambda: fetch(source, used[half], half, True).start())
                pl.when(place != source)(lambda: fetch(source, used[half], half, False).start())

        @pl.when(has_left)
        def _():
            for half in range(pair):

                @pl.when(real[half] >= 0)
                def _():
                    for source in range(line):
                        seam_arrival(source, used[half]).wait_recv()

            for half in range(pair):
                for source in range(line):
                    fetch_seam(source, used[half], half).start()

        @pl.when(chunk >= 2)
        def _():
            for step in range(1, groups):
                block_copy(step, chunk - 2).wait_send()
            own_copy(chunk - 2).wait()

        for half in range(pair):
            for source in range(line):
                fetch(source, used[half], half, False).wait()

        @pl.when(has_left)
        def _():
            for half in range(pair):
                for source in range(line):
                    fetch_seam(source, used[half], half).wait()
            render(chunk, True)

        @pl.when(jnp.logical_not(has_left))
        def _():
            render(chunk, False)

    head = line - 1 + lead
    for step in range(1 + lead):
        advance(step)
    for sender in range(line):
        pl.when(place != sender)(lambda: card_arrival(0, sender).wait_recv())
        pl.when(has_left)(lambda: card_arrival(1, sender).wait_recv())
    cards_copy = pltpu.make_async_copy(cards_v, cards, own_sem.at[0])
    cards_copy.start()
    cards_copy.wait()
    lax.fori_loop(0, groups * slots, build, 0)

    def turn(step, carry):
        advance(step)
        done = step - head + 1 + spare

        @pl.when((step >= head) & (done % pair == 0))
        def _():
            compute(done // pair - 1)

        return carry

    lax.fori_loop(1 + lead, bands + head, turn, 0)

    for other in range(line):
        pl.when(place != other)(lambda: card_copy(0, other).wait_send())
        pl.when(has_next)(lambda: card_copy(1, other).wait_send())

    def settle(band, carry):
        for way in (0, 1):
            for hop in range(line - 1):

                @pl.when(sends_to(way, hop))
                def _():
                    hop_copy(way, hop, band, hop == 0).wait_send()

        @pl.when(has_next)
        def _():
            for source in range(line):
                pl.when(place == source)(lambda: seam_copy(source, band, True).wait_send())
                pl.when(place != source)(lambda: seam_copy(source, band, False).wait_send())

        return carry

    lax.fori_loop(0, bands, settle, 0)

    def gather_in(chunk, carry):
        @pl.when(chunk >= chunks - 2)
        def _():
            for step in range(1, groups):
                block_copy(step, chunk).wait_send()
            own_copy(chunk).wait()

        for step in range(1, groups):
            block_arrival(step, chunk).wait_recv()
        return carry

    lax.fori_loop(0, chunks, gather_in, 0)


def table_kernel(
    sizes,
    seam_ref,
    source_ref,
    shift_ref,
    blend_ref,
    from_ref,
    tile_ref,
    weight_ref,
    moved_ref,
    pick_ref,
    order_ref,
    card_ref,
    counts,
):
    line, groups, slots, loc, per_owner = sizes
    seam_count = seam_ref.shape[0]
    myself = lax.axis_index("tile")
    place = myself // groups
    group = myself % groups

    def clear(slot, carry):
        from_ref[slot] = 0
        tile_ref[slot] = 0
        weight_ref[slot] = 0.0
        moved_ref[2 * slot] = 0.0
        moved_ref[2 * slot + 1] = 0.0
        return carry

    lax.fori_loop(0, groups * slots + 1, clear, 0)

    for owner in range(groups):

        def fill(index, count):
            block = (place * groups + owner) * per_owner + index
            value = source_ref[block]
            device = value // loc
            slot = owner * slots + count
            from_ref[slot] = device // groups
            tile_ref[slot] = value - device * loc
            weight_ref[slot] = blend_ref[block]
            moved_ref[2 * slot] = shift_ref[2 * block]
            moved_ref[2 * slot + 1] = shift_ref[2 * block + 1]
            return count + jnp.where(lax.rem(device, groups) == group, 1, 0)

        lax.fori_loop(0, per_owner, fill, 0)

    for sender in range(groups):
        counts[sender] = 0

    def choose(index, carry):
        sender = lax.rem(source_ref[myself * per_owner + index] // loc, groups)
        count = counts[sender]
        pick_ref[index] = sender * slots + count
        counts[sender] = count + 1
        return carry

    lax.fori_loop(0, per_owner, choose, 0)

    columns = lax.broadcasted_iota(jnp.int32, card_ref.shape, 1)
    card = jnp.zeros(card_ref.shape, jnp.int32)
    for entry in range(seam_count):
        card = jnp.where(columns == entry, seam_ref[entry], card)
    card_ref[...] = card
    for tile in range(loc):
        listed, spot, below = 0, 0, 0
        for entry in range(seam_count):
            listed = listed + jnp.where(seam_ref[entry] == tile, 1, 0)
            spot = spot + jnp.where(seam_ref[entry] == tile, entry, 0)
            below = below + jnp.where(seam_ref[entry] < tile, 1, 0)
        order_ref[jnp.where(listed > 0, spot, seam_count + tile - below)] = tile


def pick_kernel(pick_ref, incoming, out, held, in_sems, out_sems):
    spare = incoming.shape[1] - out.shape[1]

    def copy_in(block):
        return pltpu.make_async_copy(
            incoming.at[pick_ref[block], pl.ds(spare, out.shape[1])],
            held.at[block],
            in_sems.at[block],
        )

    def copy_out(block):
        return pltpu.make_async_copy(held.at[block], out.at[block], out_sems.at[block])

    def begin(block, carry):
        copy_in(block).start()
        return carry

    def relay(block, carry):
        copy_in(block).wait()
        copy_out(block).start()
        return carry

    def finish(block, carry):
        copy_out(block).wait()
        return carry

    lax.fori_loop(0, out.shape[0], begin, 0)
    lax.fori_loop(0, out.shape[0], relay, 0)
    lax.fori_loop(0, out.shape[0], finish, 0)


def local(zones, tile_count, tiles, seam_list, source, offsets, fractions, blend):
    loc, bands, height, width = tiles.shape
    seam_count = seam_list.shape[0]
    line = line_length(tile_count)
    groups = tile_count // line
    per_owner = source.shape[0] // tile_count
    capacity = max(2, 2 * per_owner // tile_count)
    slots = min(per_owner, line * capacity)
    half = (height // 2, width // 2)
    total = groups * slots
    padded = -(-bands // pair) * pair
    any_space = pl.BlockSpec(memory_space=pl.ANY)
    smem = pl.BlockSpec(memory_space=pltpu.SMEM)
    vmem = pl.BlockSpec(memory_space=pltpu.VMEM)
    kind = tiles.dtype

    shift = (offsets.astype(jnp.float32) + fractions).reshape(-1)
    came, tile, weight, moved, picks, order, card = pl.pallas_call(
        functools.partial(table_kernel, (line, groups, slots, loc, per_owner)),
        out_shape=[
            jax.ShapeDtypeStruct((total + 1,), jnp.int32),
            jax.ShapeDtypeStruct((total + 1,), jnp.int32),
            jax.ShapeDtypeStruct((total + 1,), jnp.float32),
            jax.ShapeDtypeStruct((2 * total + 2,), jnp.float32),
            jax.ShapeDtypeStruct((per_owner,), jnp.int32),
            jax.ShapeDtypeStruct((loc,), jnp.int32),
            jax.ShapeDtypeStruct((8, 128), jnp.int32),
        ],
        in_specs=[smem] * 4,
        out_specs=[smem] * 6 + [vmem],
        scratch_shapes=[pltpu.SMEM((groups,), jnp.int32)],
    )(seam_list, source, shift, blend)

    _, _, incoming = pl.pallas_call(
        functools.partial(exchange_kernel, (zones, line, groups, slots)),
        out_shape=[
            jax.ShapeDtypeStruct((bands, line, loc, height, width), kind),
            jax.ShapeDtypeStruct((bands, line, seam_count, height, width), kind),
            jax.ShapeDtypeStruct((groups, slots, padded) + half, kind),
        ],
        in_specs=[smem] * 5 + [vmem, vmem],
        out_specs=[any_space] * 3,
        scratch_shapes=[
            pltpu.VMEM((total, height // 2, height), kind),
            pltpu.VMEM((total, width, width // 2), kind),
            pltpu.VMEM((pair, line * loc, height, width), kind),
            pltpu.VMEM((pair, line * seam_count, height, width), kind),
            pltpu.VMEM((2, groups, slots, pair) + half, kind),
            pltpu.VMEM((bands, loc, height, width), kind),
            pltpu.VMEM((2, line, 8, 128), jnp.int32),
            pltpu.SMEM((2, line, 8, 128), jnp.int32),
            pltpu.SMEM((total,), jnp.int32),
            pltpu.SMEM((total,), jnp.int32),
            pltpu.SMEM((total,), jnp.float32),
            pltpu.SemaphoreType.DMA((2, line)),
            pltpu.SemaphoreType.DMA((2, line)),
            pltpu.SemaphoreType.DMA((2, line - 1, bands)),
            pltpu.SemaphoreType.DMA((2, line - 1, bands)),
            pltpu.SemaphoreType.DMA((line, bands)),
            pltpu.SemaphoreType.DMA((line, bands)),
            pltpu.SemaphoreType.DMA((groups, padded // pair)),
            pltpu.SemaphoreType.DMA((groups, padded // pair)),
            pltpu.SemaphoreType.DMA((pair, 2 * line)),
            pltpu.SemaphoreType.DMA((2,)),
        ],
        compiler_params=pltpu.CompilerParams(
            collective_id=0, has_side_effects=True, vmem_limit_bytes=52 * 1024 * 1024
        ),
    )(came, tile, weight, moved, order, card, tiles)

    return pl.pallas_call(
        pick_kernel,
        in_specs=[smem, any_space],
        out_specs=any_space,
        out_shape=jax.ShapeDtypeStruct((per_owner, bands) + half, kind),
        scratch_shapes=[
            pltpu.VMEM((per_owner, bands) + half, kind),
            pltpu.SemaphoreType.DMA((per_owner,)),
            pltpu.SemaphoreType.DMA((per_owner,)),
        ],
        compiler_params=pltpu.CompilerParams(vmem_limit_bytes=56 * 1024 * 1024),
    )(picks, incoming.reshape((total, padded) + half))


def solution(mesh):
    in_specs = (
        P(("zone", "tile"), None, None, None),
        P(("zone", "tile")),
        P("zone"),
        P("zone", None),
        P("zone", None),
        P("zone"),
    )
    out_specs = P(("zone", "tile"), None, None, None)
    body = functools.partial(local, mesh.shape["zone"], mesh.shape["tile"])
    return jax.shard_map(body, mesh=mesh, in_specs=in_specs, out_specs=out_specs, check_vma=False)
```
